768 devices in a mesh: dp: 24 (over z, core), group: 32 (over y, x).
Axes of the slice: x: 4, y: 8, z: 12, core: 2. Of those that a mesh axis runs over, the one named last changes fastest.
Arguments:
- embeddings: bfloat16 [98304, 1024], P(('dp', 'group'))
- coarse_lists: int32 [6144, 4], P(('dp', 'group')), may hold values from 0 to 23, all different within a row; in each aligned block of 8 rows (0 to 7, 8 to 15, ...) at most 2 rows name the same one
- home: int32 [32, 24], P('group'), may hold values from 0 to 23, each once within a row
- centroids: bfloat16 [32, 24, 256, 1024], P('group', 'dp')
Outputs:
- new_centroids: float32 [32, 24, 256, 1024], P('group', 'dp')
- weights: float32 [32, 24, 256], P('group', 'dp')
The draws below stay inside these ranges and needn't reach their ends.
Inputs may be any that keep to these rules, and one draw needn't show every extreme that they name: `coarse_lists`: each row names 4 different block numbers; among the slabs of one device no block number is named more than 2 times. `home`: each row is a permutation.
All inputs are finite; a program needn't handle non-finite values.
Results may differ from the reference program's by a relative error of at most 0.013.
Values may be sent and summed in bfloat16 or wider, within the bound.
No kernel may reach another device: no remote copies, remote signals or barrier semaphores. Data moves between devices by JAX's collectives and lax.ppermute only.
A program may use at most 32 MiB of HBM per device.

```python
import math
import jax
import jax.numpy as jnp
import numpy as np
from jax import lax

D = 1024
BLK = 256
ROWS = 128
SLAB = 16
LIST = 4
ITERS = 2
MOST = 2
TOKENS = 98304
N_DP = 24
N_GROUP = 32


def common_direction(key):
    return jnp.clip(jax.random.normal(jax.random.fold_in(key, 5), (D,), jnp.float32), -2.5, 2.5)


def draw_embeddings(key, part):
    direction = common_direction(key)
    key = jax.random.fold_in(key, 11)
    first_key = jax.random.fold_in(key, 0)
    second_key = jax.random.fold_in(key, 1)
    fourth_key = jax.random.fold_in(key, 3)
    fifth_key = jax.random.fold_in(key, 4)
    positions = jnp.arange(TOKENS, dtype=jnp.float32)
    rising = jnp.exp(jnp.log(3.0) * positions / TOKENS)[:, None]
    rough = jnp.exp(jax.random.uniform(second_key, (TOKENS, 1), jnp.float32, 0.0, jnp.log(10.0)))
    base = jnp.clip(jax.random.normal(first_key, (TOKENS, D), jnp.float32), -6.0, 6.0)
    typical = base * rough
    chosen = jax.random.bernoulli(fourth_key, 1.0 / 16.0, (TOKENS, 1))
    strength = jax.random.uniform(fifth_key, (TOKENS, 1), jnp.float32, 1.0, 3.0)
    aligned = 9.0 * strength * direction[None, :] + base
    values = jnp.where(chosen, aligned, typical) * rising
    return values.astype(jnp.bfloat16)


def draw_centroids(key, part):
    direction = common_direction(key)
    key = jax.random.fold_in(key, 13)

    def group_draw(index):
        group_key = jax.random.fold_in(key, index)
        noise_key, pick_key, beta_key = jax.random.split(group_key, 3)
        noise = jnp.clip(jax.random.normal(noise_key, (N_DP, BLK, D), jnp.float32), -6.0, 6.0)
        strength = jax.random.uniform(beta_key, (N_DP, BLK, 1), jnp.float32, 1.5, 4.0)
        chosen = jax.random.bernoulli(pick_key, 4.0 / BLK, (N_DP, BLK, 1))
        values = noise + jnp.where(chosen, strength, 0.0) * direction[None, None, :]
        return values.astype(jnp.bfloat16)
    return lax.map(group_draw, jnp.arange(N_GROUP, dtype=jnp.int32))


def assign_block(stream_key, own, number, rows, number_of, top, bound, lean):
    ranking = jax.random.permutation(stream_key, number_of)
    heavy_load, usual = portions_of(number_of, rows * top, bound, lean, True), portions_of(number_of, rows * top, bound, lean, False)
    places = jnp.arange(number_of)

    def named(sizes, offset_by):
        used = int((sizes > 0).sum())
        fixed = max(1, used // 4)
        moved = fixed + (places - fixed + offset_by * (used - fixed)) % max(1, number_of - fixed)
        return jnp.zeros((number_of,), jnp.int32).at[ranking[jnp.where(places < fixed, places, moved)]].set(jnp.asarray(sizes, jnp.int32))

    sizes = jnp.where(number % 4 == 0, named(heavy_load, number // 4), named(usual, number - number // 4 - 1))
    mixed = jax.random.permutation(jax.random.fold_in(own, 3), number_of)
    source_of, taker = mixed[0:number_of // 2 * 2:2], mixed[1:number_of // 2 * 2:2]
    margin = jnp.minimum(sizes[source_of] - 1, bound - sizes[taker]) // 2
    margin = jnp.where((source_of == ranking[0]) | (taker == ranking[0]) | (sizes[taker] == 0), 0, jnp.maximum(margin, 0))
    moved = jax.random.randint(jax.random.fold_in(own, 4), (number_of // 2,), 0, 1 << 20) % (margin + 1)
    sizes = sizes.at[source_of].add(-moved).at[taker].add(moved)
    items = jnp.searchsorted(jnp.cumsum(sizes), jnp.arange(rows * top), side="right").astype(jnp.int32)
    table = items.reshape(top, rows).T
    table = table[jax.random.permutation(jax.random.fold_in(own, 1), rows)]
    offset_by = jax.random.randint(jax.random.fold_in(own, 2), (rows, 1), 0, top)
    return jnp.take_along_axis(table, (jnp.arange(top)[None, :] + offset_by) % top, axis=1)


def portions_of(count, total, bound, slope, full):
    portions = [(1 << 20) // math.isqrt(standing ** slope) + 1 for standing in range(1, count + 1)]
    largest = bound if full else min(bound, max(-(-total // count), total * portions[0] // sum(portions)))
    least = 1 if total - largest >= count - 1 else 0
    counts, spare = [largest] + [least] * (count - 1), total - largest - least * (count - 1)
    while spare > 0:
        free = [i for i in range(1, count) if counts[i] < largest] or [i for i in range(1, count) if counts[i] < bound]
        mass, left = sum([portions[i] for i in free]), spare
        for i in free:
            addition = min(bound - counts[i], max(1, left * portions[i] // mass), spare)
            counts[i] = counts[i] + addition
            spare = spare - addition
    return np.array(counts)


def setup_inputs(seed: int = 0) -> dict:
    splits = jax.random.split(jax.random.key(seed), 5)
    embeddings = draw_embeddings(jax.random.fold_in(splits[4], 71), 0)
    coarse_lists_keys = jax.random.split(jax.random.fold_in(splits[1], 1), (TOKENS // SLAB) // (ROWS // SLAB))
    coarse_lists_turns = jax.random.permutation(jax.random.fold_in(splits[1], 3), (TOKENS // SLAB) // (ROWS // SLAB))
    coarse_lists = jax.vmap(lambda own, number: assign_block(jax.random.fold_in(splits[1], 2), own, number, ROWS // SLAB, N_DP, LIST, MOST, 2))(coarse_lists_keys, coarse_lists_turns).reshape((TOKENS // SLAB, LIST))
    home = jax.vmap(lambda own: jax.random.permutation(own, N_DP))(jax.random.split(splits[2], N_GROUP)).reshape((N_GROUP, N_DP)).astype(jnp.int32)
    centroids = draw_centroids(jax.random.fold_in(splits[4], 71), 0)
    return dict(embeddings=embeddings, coarse_lists=coarse_lists, home=home, centroids=centroids)


prior_count = 1.0

def one_group(operands):
    group_rows, group_lists, home_row, group_cent = operands
    positions = jnp.arange(N_DP, dtype=jnp.int32)
    slots = lax.optimization_barrier(jnp.sum(jnp.where(group_lists[:, :, None] == positions, home_row, 0), axis=2))
    listed = jnp.any(slots[:, :, None] == positions, axis=1)
    row_listed = jnp.repeat(listed, SLAB, axis=0)[:, :, None]
    rows_float = group_rows.astype(jnp.float32)
    current = group_cent.astype(jnp.float32)
    weight_sum = jnp.zeros((N_DP, BLK), jnp.float32)
    for turn_index in range(ITERS):
        block_low = lax.optimization_barrier(current.astype(jnp.bfloat16)).astype(jnp.float32)
        cnorm = lax.optimization_barrier(jnp.sum(block_low * block_low, axis=2))
        logits = (2.0 * jnp.einsum('rd,pjd->rpj', rows_float, block_low) - cnorm[None]) / math.sqrt(D)
        masked = jnp.where(row_listed, logits, -jnp.inf)
        normal_total = jax.nn.logsumexp(masked, axis=(1, 2))
        resp = jnp.where(row_listed, jnp.exp(masked - normal_total[:, None, None]), 0.0)
        weight_sum = lax.optimization_barrier(jnp.sum(resp, axis=0))
        resp_low = lax.optimization_barrier(resp.astype(jnp.bfloat16)).astype(jnp.float32)
        sums = jnp.einsum('rpj,rd->pjd', resp_low, rows_float)
        current = (sums + current) / (weight_sum[:, :, None] + prior_count)
    return (current, weight_sum)

def reference(embeddings, coarse_lists, home, centroids):
    values = embeddings.astype(jnp.float32)
    squares = lax.optimization_barrier(jnp.sum(values * values, axis=0))
    feature_scale = lax.rsqrt(squares / TOKENS + 1e-06)
    standard = (values * feature_scale).astype(jnp.bfloat16)
    by_group = standard.reshape(N_DP, N_GROUP, ROWS, D).transpose(1, 0, 2, 3).reshape(N_GROUP, N_DP * ROWS, D)
    lists_group = coarse_lists.reshape(N_DP, N_GROUP, ROWS // SLAB, LIST).transpose(1, 0, 2, 3).reshape(N_GROUP, N_DP * (ROWS // SLAB), LIST)
    new_centroids, weights = lax.map(one_group, (by_group, lists_group, home, centroids))
    return (new_centroids, weights)
```

```python
import math

import jax
import jax.numpy as jnp
import numpy as np
from jax import lax
from jax.experimental import pallas as pl
from jax.experimental.pallas import tpu as pltpu
from jax.sharding import Mesh, PartitionSpec as P

ITERS = 2
DP = ("z", "core")
LANES = 128

prior_count = 1.0


def vmem(count):
    return [pl.BlockSpec(memory_space=pltpu.VMEM)] * count


def call(body, outs, specs, flops, moved):
    return pl.pallas_call(
        body,
        out_shape=outs,
        in_specs=specs,
        out_specs=tuple(vmem(len(outs))),
        compiler_params=pltpu.CompilerParams(vmem_limit_bytes=40 * 2**20),
        cost_estimate=pl.CostEstimate(flops=flops, bytes_accessed=moved, transcendentals=0),
    )


def dispatch(slab_rows, most, peers, lists_ref, home_ref, emb_ref, out_ref, table):
    slabs, listed = lists_ref.shape

    def clear(p, carry):
        table[p] = 0
        return carry

    lax.fori_loop(0, peers * most, clear, 0)

    def count_clear(p, carry):
        table[peers * most + p] = 0
        return carry

    lax.fori_loop(0, peers, count_clear, 0)

    def place(n, carry):
        slab, k = n // listed, n % listed
        p = home_ref[0, lists_ref[slab, k]]
        seen = table[peers * most + p]
        table[p * most + jnp.minimum(seen, most - 1)] = slab
        table[peers * most + p] = seen + 1
        return carry

    lax.fori_loop(0, slabs * listed, place, 0)

    def copy(n, carry):
        source = pl.multiple_of(table[n] * slab_rows, slab_rows)
        target = pl.multiple_of(n * slab_rows, slab_rows)
        out_ref[pl.ds(target, slab_rows), :] = emb_ref[pl.ds(source, slab_rows), :]
        return carry

    lax.fori_loop(0, peers * most, copy, 0)


def block_stats(block_low, std_ref, logits_ref, stat_ref):
    width = block_low.shape[1]
    peers, rows, lanes = stat_ref.shape
    wide = block_low.astype(jnp.float32)
    cnorm = jnp.sum(wide * wide, axis=1, keepdims=True)
    chunk = 2 * lanes
    lines = []
    for c in range(std_ref.shape[0] // chunk):
        products = lax.dot_general(
            block_low,
            std_ref[c * chunk : (c + 1) * chunk, :],
            (((1,), (1,)), ((), ())),
            preferred_element_type=jnp.float32,
        )
        logits = (2.0 * products - cnorm) * (1.0 / math.sqrt(width))
        logits_ref[:, c * chunk : (c + 1) * chunk] = logits
        largest = jnp.max(logits, axis=0, keepdims=True)
        total = jnp.sum(jnp.exp(logits - largest), axis=0, keepdims=True)
        both = largest + jnp.log(total)
        lines += [both[:, h * lanes : (h + 1) * lanes] for h in range(2)]
    lines += [jnp.zeros((1, lanes), jnp.float32)] * (rows - len(lines))
    stat = jnp.concatenate(lines, axis=0)
    for p in range(peers):
        stat_ref[p] = stat


def first_body(got_ref, scale_ref, block_ref, std_ref, logits_ref, stat_ref):
    chunk = 2 * LANES
    scale = scale_ref[...]
    for c in range(got_ref.shape[0] // chunk):
        at = slice(c * chunk, (c + 1) * chunk)
        std_ref[at, :] = (got_ref[at, :].astype(jnp.float32) * scale).astype(jnp.bfloat16)
    block_stats(block_ref[...], std_ref, logits_ref, stat_ref)


def combine(stats_ref, same_ref, swap_ref, slab_rows):
    peers, rows, lanes = stats_ref.shape
    own = stats_ref[...].reshape(peers * rows, lanes)
    lane = lax.broadcasted_iota(jnp.int32, own.shape, 1)
    ahead = pltpu.roll(own, lanes - slab_rows, 1)
    behind = pltpu.roll(own, slab_rows, 1)
    other = jnp.where(lane % (2 * slab_rows) < slab_rows, ahead, behind)
    own = own.reshape(peers, rows, lanes)
    other = other.reshape(peers, rows, lanes)
    first = jnp.where(same_ref[...] > 0, own, -jnp.inf)
    second = jnp.where(swap_ref[...] > 0, other, -jnp.inf)
    summit = jnp.max(jnp.maximum(first, second), axis=0)
    live = summit > -jnp.inf
    summit = jnp.where(live, summit, 0.0)
    total = jnp.sum(jnp.exp(first - summit) + jnp.exp(second - summit), axis=0)
    return jnp.where(live, summit + jnp.log(jnp.where(live, total, 1.0)), jnp.inf)


def update(normal, logits_ref, std_ref, old):
    lanes = normal.shape[1]
    parts = []
    for r in range(logits_ref.shape[1] // lanes):
        parts.append(jnp.exp(logits_ref[:, r * lanes : (r + 1) * lanes] - normal[r : r + 1, :]))
    resp = jnp.concatenate(parts, axis=1)
    weight = jnp.sum(resp, axis=1, keepdims=True)
    sums = lax.dot_general(
        resp.astype(jnp.bfloat16),
        std_ref[...],
        (((1,), (0,)), ((), ())),
        preferred_element_type=jnp.float32,
    )
    return (sums + old) / (weight + prior_count), weight


def middle_body(
    slab_rows, stats_ref, same_ref, swap_ref, logits_ref, std_ref, old_ref, new_ref, next_ref, stat_ref
):
    normal = combine(stats_ref, same_ref, swap_ref, slab_rows)
    current, _ = update(normal, logits_ref, std_ref, old_ref[...].astype(jnp.float32))
    new_ref[...] = current
    block_stats(current.astype(jnp.bfloat16), std_ref, next_ref, stat_ref)


def last_body(
    slab_rows, stats_ref, same_ref, swap_ref, logits_ref, std_ref, old_ref, new_ref, weight_ref
):
    normal = combine(stats_ref, same_ref, swap_ref, slab_rows)
    current, weight = update(normal, logits_ref, std_ref, old_ref[...].astype(jnp.float32))
    new_ref[...] = current
    flat = jnp.transpose(jnp.broadcast_to(weight, (weight.shape[0], LANES)))
    weight_ref[...] = flat[:1, :]


def spread(x):
    return lax.all_to_all(x, DP, split_axis=0, concat_axis=0, tiled=True)


def per_device(embeddings, coarse_lists, home, centroids):
    row_count, width = embeddings.shape
    peers = lax.axis_size(DP)
    total_rows = row_count * peers * lax.axis_size(("y", "x"))
    slabs, listed = coarse_lists.shape
    slab_rows = row_count // slabs
    most = 2
    slots = peers * most * slab_rows
    f32 = jnp.float32

    with jax.named_scope("sums_and_lists"):
        squares = jnp.sum(jnp.square(embeddings.astype(f32)), axis=0).reshape(-1, LANES)
        names = jnp.pad(coarse_lists.reshape(1, -1).astype(f32), ((0, 0), (0, LANES - slabs * listed)))
        payload = jnp.concatenate([squares, names], axis=0)
        shared = spread(jnp.broadcast_to(payload[None], (peers, *payload.shape)))

    with jax.named_scope("slabs_out"):
        outgoing = pl.pallas_call(
            lambda *refs: dispatch(slab_rows, most, peers, *refs),
            out_shape=jax.ShapeDtypeStruct((slots, width), jnp.bfloat16),
            in_specs=[pl.BlockSpec(memory_space=pltpu.SMEM)] * 2 + vmem(1),
            out_specs=vmem(1)[0],
            scratch_shapes=[pltpu.SMEM((peers * (most + 1),), jnp.int32)],
        )(coarse_lists, home, embeddings)
        received = spread(outgoing.reshape(peers, most * slab_rows, width)).reshape(slots, width)

    with jax.named_scope("feature_scale"):
        total = jnp.sum(shared[:, : width // LANES], axis=0)
        total = lax.psum(lax.psum(total, "x"), "y")
        scale = lax.rsqrt(total / total_rows + 1e-06).reshape(1, width)

    with jax.named_scope("slot_masks"):
        me = lax.axis_index(DP)
        ids = jnp.arange(peers, dtype=jnp.int32)
        lists_all = shared[:, width // LANES, : slabs * listed].astype(jnp.int32)
        home_of = jnp.sum(jnp.where(lists_all[:, :, None] == ids, home[0], 0), axis=2)
        hits = jnp.any(home_of.reshape(peers, slabs, listed)[..., None] == ids, axis=2)
        order = jnp.arange(slabs)
        earlier = (order[None, :] < order[:, None])[None, :, :, None]
        before = jnp.sum(jnp.where(earlier & hits[:, None], 1, 0), axis=2)
        place = jnp.where(hits, before, -1)
        mine = jnp.sum(jnp.where(ids == me, place, 0), axis=2)
        turn = jnp.arange(most)
        chosen = mine[:, None, :] == turn[:, None]

        def lanes_of(wanted):
            found = chosen[..., None] & (place[:, None] == wanted[:, None, None])
            found = jnp.any(found, axis=2).astype(f32)
            found = found.transpose(2, 0, 1).reshape(peers, peers * most)
            found = jnp.repeat(found, slab_rows, axis=1).reshape(peers, -1, LANES)
            return jnp.pad(found, ((0, 0), (0, -found.shape[1] % 8), (0, 0)))

        same, swap = lanes_of(turn), lanes_of(1 - turn)

    block = centroids[0, 0]
    rows_of_stat = same.shape[1]
    work = 2 * slots * block.shape[0] * width
    logits_shape = jax.ShapeDtypeStruct((block.shape[0], slots), f32)
    stat_shape = jax.ShapeDtypeStruct((peers, rows_of_stat, LANES), f32)
    block_shape = jax.ShapeDtypeStruct(block.shape, f32)
    with jax.named_scope("first_logits"):
        std, logits, stat = call(
            first_body,
            (jax.ShapeDtypeStruct((slots, width), jnp.bfloat16), logits_shape, stat_shape),
            vmem(3),
            work,
            4 << 20,
        )(received, scale, block)
    old = block
    for turn_index in range(ITERS - 1):
        with jax.named_scope("stats_out"):
            stats = spread(stat)
        with jax.named_scope("middle_update"):
            old, logits, stat = call(
                lambda *refs: middle_body(slab_rows, *refs),
                (block_shape, logits_shape, stat_shape),
                vmem(6),
                2 * work,
                5 << 20,
            )(stats, same, swap, logits, std, old)
    with jax.named_scope("last_stats_out"):
        stats = spread(stat)
    with jax.named_scope("last_update"):
        current, weight = call(
            lambda *refs: last_body(slab_rows, *refs),
            (block_shape, jax.ShapeDtypeStruct((1, block.shape[0]), f32)),
            vmem(6),
            work,
            5 << 20,
        )(stats, same, swap, logits, std, old)
    return current[None, None], weight[None]


def solution(mesh):
    chips, rows = 12, 8
    grid = np.asarray(mesh.devices).reshape(chips, mesh.devices.shape[0] // chips, rows, -1)
    fine = Mesh(grid, ("z", "core", "y", "x"))
    group = ("y", "x")
    return jax.shard_map(
        per_device,
        mesh=fine,
        in_specs=(P(DP + group, None), P(DP + group, None), P(group, None), P(group, DP, None, None)),
        out_specs=(P(group, DP, None, None), P(group, DP, None)),
        check_vma=False,
    )
```

```python
import math

import jax
import jax.numpy as jnp
import numpy as np
from jax import lax
from jax.experimental import pallas as pl
from jax.experimental.pallas import tpu as pltpu
from jax.sharding import Mesh, PartitionSpec as P

ITERS = 2
DP = ("z", "core")
LANES = 128

prior_count = 1.0


def vmem(count):
    return [pl.BlockSpec(memory_space=pltpu.VMEM)] * count


def call(body, outs, specs, flops, moved):
    return pl.pallas_call(
        body,
        out_shape=outs,
        in_specs=specs,
        out_specs=tuple(vmem(len(outs))),
        compiler_params=pltpu.CompilerParams(vmem_limit_bytes=16 * 2**20),
        cost_estimate=pl.CostEstimate(flops=flops, bytes_accessed=moved, transcendentals=0),
    )


def share_body(lists_ref, emb_ref, out_ref):
    listed, slabs = lists_ref.shape
    wide = emb_ref[...].astype(jnp.float32)
    squares = jnp.sum(wide * wide, axis=0, keepdims=True)
    lines = [squares[:, c : c + LANES] for c in range(0, wide.shape[1], LANES)]
    lane = lax.broadcasted_iota(jnp.int32, (1, LANES), 1)
    names = jnp.zeros((1, LANES), jnp.int32)
    for n in range(slabs * listed):
        names = jnp.where(lane == n, lists_ref[n % listed, n // listed], names)
    payload = jnp.concatenate([*lines, names.astype(jnp.float32)], axis=0)
    for p in range(out_ref.shape[0]):
        out_ref[p] = payload


def dispatch(slab_rows, most, peers, lists_ref, home_ref, emb_ref, out_ref, table):
    listed, slabs = lists_ref.shape

    def clear(p, carry):
        table[p] = 0
        return carry

    lax.fori_loop(0, peers * most, clear, 0)

    def count_clear(p, carry):
        table[peers * most + p] = 0
        return carry

    lax.fori_loop(0, peers, count_clear, 0)

    def place(n, carry):
        slab, k = n // listed, n % listed
        p = home_ref[0, lists_ref[k, slab]]
        seen = table[peers * most + p]
        table[p * most + jnp.minimum(seen, most - 1)] = slab
        table[peers * most + p] = seen + 1
        return carry

    lax.fori_loop(0, slabs * listed, place, 0)

    def copy(n, carry):
        source = pl.multiple_of(table[n] * slab_rows, slab_rows)
        target = pl.multiple_of(n * slab_rows, slab_rows)
        out_ref[pl.ds(target, slab_rows), :] = emb_ref[pl.ds(source, slab_rows), :]
        return carry

    lax.fori_loop(0, peers * most, copy, 0)


def block_logits(block_low, std_ref):
    width = block_low.shape[1]
    wide = block_low.astype(jnp.float32)
    cnorm = jnp.sum(wide * wide, axis=1, keepdims=True)
    chunk = 2 * LANES
    for c in range(0, std_ref.shape[0], chunk):
        products = lax.dot_general(
            block_low,
            std_ref[c : c + chunk, :],
            (((1,), (1,)), ((), ())),
            preferred_element_type=jnp.float32,
        )
        yield c, chunk, (2.0 * products - cnorm) * (1.0 / math.sqrt(width))


def block_stats(block_low, std_ref, stat_ref, logits_ref=None):
    peers, rows, lanes = stat_ref.shape
    lines = []
    for c, chunk, logits in block_logits(block_low, std_ref):
        if logits_ref is not None:
            logits_ref[:, c : c + chunk] = logits
        largest = jnp.max(logits, axis=0, keepdims=True)
        total = jnp.sum(jnp.exp(logits - largest), axis=0, keepdims=True)
        both = largest + jnp.log(total)
        lines += [both[:, h * lanes : (h + 1) * lanes] for h in range(2)]
    lines += [jnp.zeros((1, lanes), jnp.float32)] * (rows - len(lines))
    stat = jnp.concatenate(lines, axis=0)
    for p in range(peers):
        stat_ref[p] = stat


def first_body(got_ref, scale_ref, block_ref, std_ref, stat_ref):
    chunk = 2 * LANES
    scale = jnp.concatenate([scale_ref[r : r + 1, :] for r in range(scale_ref.shape[0])], axis=1)
    for c in range(got_ref.shape[0] // chunk):
        at = slice(c * chunk, (c + 1) * chunk)
        std_ref[at, :] = (got_ref[at, :].astype(jnp.float32) * scale).astype(jnp.bfloat16)
    block_stats(block_ref[...], std_ref, stat_ref)


def combine(stats_ref, same_ref, swap_ref, slab_rows):
    peers, rows, lanes = stats_ref.shape
    own = stats_ref[...].reshape(peers * rows, lanes)
    lane = lax.broadcasted_iota(jnp.int32, own.shape, 1)
    ahead = pltpu.roll(own, lanes - slab_rows, 1)
    behind = pltpu.roll(own, slab_rows, 1)
    other = jnp.where(lane % (2 * slab_rows) < slab_rows, ahead, behind)
    own = own.reshape(peers, rows, lanes)
    other = other.reshape(peers, rows, lanes)
    first = jnp.where(same_ref[...] > 0, own, -jnp.inf)
    second = jnp.where(swap_ref[...] > 0, other, -jnp.inf)
    summit = jnp.max(jnp.maximum(first, second), axis=0)
    live = summit > -jnp.inf
    summit = jnp.where(live, summit, 0.0)
    total = jnp.sum(jnp.exp(first - summit) + jnp.exp(second - summit), axis=0)
    return jnp.where(live, summit + jnp.log(jnp.where(live, total, 1.0)), jnp.inf)


def update(normal, logits, std_ref, old):
    parts = []
    for c, chunk, values in logits:
        for h in range(0, chunk, LANES):
            r = (c + h) // LANES
            parts.append(jnp.exp(values[:, h : h + LANES] - normal[r : r + 1, :]))
    resp = jnp.concatenate(parts, axis=1)
    weight = jnp.sum(resp, axis=1, keepdims=True)
    sums = lax.dot_general(
        resp.astype(jnp.bfloat16),
        std_ref[...],
        (((1,), (0,)), ((), ())),
        preferred_element_type=jnp.float32,
    )
    return (sums + old) / (weight + prior_count), weight


def middle_body(
    slab_rows,
    stats_ref,
    same_ref,
    swap_ref,
    std_ref,
    old_ref,
    new_ref,
    next_ref,
    stat_ref,
):
    normal = combine(stats_ref, same_ref, swap_ref, slab_rows)
    old = old_ref[...]
    logits = block_logits(old.astype(jnp.bfloat16), std_ref)
    current, _ = update(normal, logits, std_ref, old.astype(jnp.float32))
    new_ref[...] = current
    block_stats(current.astype(jnp.bfloat16), std_ref, stat_ref, next_ref)


def last_body(
    slab_rows, stats_ref, same_ref, swap_ref, logits_ref, std_ref, old_ref, new_ref, weight_ref
):
    normal = combine(stats_ref, same_ref, swap_ref, slab_rows)
    logits = [(0, logits_ref.shape[1], logits_ref[...])]
    current, weight = update(normal, logits, std_ref, old_ref[...])
    new_ref[...] = current
    flat = jnp.transpose(jnp.broadcast_to(weight, (weight.shape[0], LANES)))
    weight_ref[...] = flat[:1, :]


def spread(x):
    return lax.all_to_all(x, DP, split_axis=0, concat_axis=0, tiled=True)


def per_device(embeddings, coarse_lists, home, centroids):
    row_count, width = embeddings.shape
    peers = lax.axis_size(DP)
    total_rows = row_count * peers * lax.axis_size(("y", "x"))
    slabs, listed = coarse_lists.shape
    slab_rows = row_count // slabs
    most = 2
    slots = peers * most * slab_rows
    f32 = jnp.float32

    with jax.named_scope("sums_and_lists"):
        lists = coarse_lists.T
        payload = pl.pallas_call(
            share_body,
            out_shape=jax.ShapeDtypeStruct((peers, width // LANES + 1, LANES), f32),
            in_specs=[pl.BlockSpec(memory_space=pltpu.SMEM)] + vmem(1),
            out_specs=vmem(1)[0],
        )(lists, embeddings)
        shared = spread(payload)

    with jax.named_scope("slabs_out"):
        outgoing = pl.pallas_call(
            lambda *refs: dispatch(slab_rows, most, peers, *refs),
            out_shape=jax.ShapeDtypeStruct((slots, width), jnp.bfloat16),
            in_specs=[pl.BlockSpec(memory_space=pltpu.SMEM)] * 2 + vmem(1),
            out_specs=vmem(1)[0],
            scratch_shapes=[pltpu.SMEM((peers * (most + 1),), jnp.int32)],
        )(lists, home, embeddings)
        received = spread(outgoing.reshape(peers, most * slab_rows, width)).reshape(slots, width)

    with jax.named_scope("feature_scale"):
        total = jnp.sum(shared[:, : width // LANES], axis=0)
        total = lax.psum(lax.psum(total, "x"), "y")
        scale = lax.rsqrt(total / total_rows + 1e-06)

    with jax.named_scope("slot_masks"):
        me = lax.axis_index(DP)
        ids = jnp.arange(peers, dtype=jnp.int32)
        lists_all = shared[:, width // LANES, : slabs * listed].astype(jnp.int32)
        home_of = jnp.sum(jnp.where(lists_all[:, :, None] == ids, home[0], 0), axis=2)
        hits = jnp.any(home_of.reshape(peers, slabs, listed)[..., None] == ids, axis=2)
        order = jnp.arange(slabs)
        earlier = (order[None, :] < order[:, None])[None, :, :, None]
        before = jnp.sum(jnp.where(earlier & hits[:, None], 1, 0), axis=2)
        place = jnp.where(hits, before, -1)
        mine = jnp.sum(jnp.where(ids == me, place, 0), axis=2)
        turn = jnp.arange(most)
        chosen = mine[:, None, :] == turn[:, None]

        def lanes_of(wanted):
            found = chosen[..., None] & (place[:, None] == wanted[:, None, None])
            found = jnp.any(found, axis=2).astype(f32)
            found = found.transpose(2, 0, 1).reshape(peers, peers * most)
            found = jnp.repeat(found, slab_rows, axis=1).reshape(peers, -1, LANES)
            return jnp.pad(found, ((0, 0), (0, -found.shape[1] % 8), (0, 0)))

        same, swap = lanes_of(turn), lanes_of(1 - turn)

    block = centroids[0, 0]
    rows_of_stat = same.shape[1]
    work = 2 * slots * block.shape[0] * width
    logits_shape = jax.ShapeDtypeStruct((block.shape[0], slots), f32)
    stat_shape = jax.ShapeDtypeStruct((peers, rows_of_stat, LANES), f32)
    block_shape = jax.ShapeDtypeStruct(block.shape, f32)
    with jax.named_scope("first_logits"):
        std, stat = call(
            first_body,
            (jax.ShapeDtypeStruct((slots, width), jnp.bfloat16), stat_shape),
            vmem(3),
            work,
            4 << 20,
        )(received, scale, block)
    old = block
    for turn_index in range(ITERS - 1):
        with jax.named_scope("stats_out"):
            stats = spread(stat)
        with jax.named_scope("middle_update"):
            old, logits, stat = call(
                lambda *refs: middle_body(slab_rows, *refs),
                (block_shape, logits_shape, stat_shape),
                vmem(5),
                3 * work,
                5 << 20,
            )(stats, same, swap, std, old)
    with jax.named_scope("last_stats_out"):
        stats = spread(stat)
    with jax.named_scope("last_update"):
        current, weight = call(
            lambda *refs: last_body(slab_rows, *refs),
            (block_shape, jax.ShapeDtypeStruct((1, block.shape[0]), f32)),
            vmem(6),
            work,
            5 << 20,
        )(stats, same, swap, logits, std, old)
    return current[None, None], weight[None]


def solution(mesh):
    chips, rows = 12, 8
    grid = np.asarray(mesh.devices).reshape(chips, mesh.devices.shape[0] // chips, rows, -1)
    fine = Mesh(grid, ("z", "core", "y", "x"))
    group = ("y", "x")
    return jax.shard_map(
        per_device,
        mesh=fine,
        in_specs=(P(DP + group, None), P(DP + group, None), P(group, None), P(group, DP, None, None)),
        out_specs=(P(group, DP, None, None), P(group, DP, None)),
        check_vma=False,
    )
```

```python
import math

import jax
import jax.numpy as jnp
import numpy as np
from jax import lax
from jax.experimental import pallas as pl
from jax.experimental.pallas import tpu as pltpu
from jax.sharding import Mesh, PartitionSpec as P

ITERS = 2
DP = ("z", "core")
LANES = 128

prior_count = 1.0


def vmem(count):
    return [pl.BlockSpec(memory_space=pltpu.VMEM)] * count


def call(body, outs, specs, flops, moved):
    return pl.pallas_call(
        body,
        out_shape=outs,
        in_specs=specs,
        out_specs=tuple(vmem(len(outs))),
        compiler_params=pltpu.CompilerParams(vmem_limit_bytes=16 * 2**20),
        cost_estimate=pl.CostEstimate(flops=flops, bytes_accessed=moved, transcendentals=0),
    )


def share_body(lists_ref, emb_ref, out_ref):
    listed, slabs = lists_ref.shape
    wide = emb_ref[...].astype(jnp.float32)
    squares = jnp.sum(wide * wide, axis=0, keepdims=True)
    lines = [squares[:, c : c + LANES] for c in range(0, wide.shape[1], LANES)]
    lane = lax.broadcasted_iota(jnp.int32, (1, LANES), 1)
    names = jnp.zeros((1, LANES), jnp.int32)
    for n in range(slabs * listed):
        names = jnp.where(lane == n, lists_ref[n % listed, n // listed], names)
    payload = jnp.concatenate([*lines, names.astype(jnp.float32)], axis=0)
    for p in range(out_ref.shape[0]):
        out_ref[p] = payload


def dispatch(slab_rows, most, peers, lists_ref, home_ref, emb_ref, out_ref, table):
    listed, slabs = lists_ref.shape

    def clear(p, carry):
        table[p] = 0
        return carry

    lax.fori_loop(0, peers * most, clear, 0)

    def count_clear(p, carry):
        table[peers * most + p] = 0
        return carry

    lax.fori_loop(0, peers, count_clear, 0)

    def place(n, carry):
        slab, k = n // listed, n % listed
        p = home_ref[0, lists_ref[k, slab]]
        seen = table[peers * most + p]
        table[p * most + jnp.minimum(seen, most - 1)] = slab
        table[peers * most + p] = seen + 1
        return carry

    lax.fori_loop(0, slabs * listed, place, 0)

    def copy(n, carry):
        source = pl.multiple_of(table[n] * slab_rows, slab_rows)
        target = pl.multiple_of(n * slab_rows, slab_rows)
        out_ref[pl.ds(target, slab_rows), :] = emb_ref[pl.ds(source, slab_rows), :]
        return carry

    lax.fori_loop(0, peers * most, copy, 0)


def block_logits(block_low, std_ref):
    width = block_low.shape[1]
    wide = block_low.astype(jnp.float32)
    cnorm = jnp.sum(wide * wide, axis=1, keepdims=True)
    chunk = 2 * LANES
    for c in range(0, std_ref.shape[0], chunk):
        products = lax.dot_general(
            block_low,
            std_ref[c : c + chunk, :],
            (((1,), (1,)), ((), ())),
            preferred_element_type=jnp.float32,
        )
        yield c, chunk, (2.0 * products - cnorm) * (1.0 / math.sqrt(width))


def block_stats(block_low, std_ref, stat_ref, logits_ref=None):
    peers, rows, lanes = stat_ref.shape
    lines = []
    for c, chunk, logits in block_logits(block_low, std_ref):
        if logits_ref is not None:
            logits_ref[:, c : c + chunk] = logits
        largest = jnp.max(logits, axis=0, keepdims=True)
        total = jnp.sum(jnp.exp(logits - largest), axis=0, keepdims=True)
        both = largest + jnp.log(total)
        lines += [both[:, h * lanes : (h + 1) * lanes] for h in range(2)]
    lines += [jnp.zeros((1, lanes), jnp.float32)] * (rows - len(lines))
    stat = jnp.concatenate(lines, axis=0)
    for p in range(peers):
        stat_ref[p] = stat


def first_body(got_ref, scale_ref, block_ref, same_ref, swap_ref, std_ref, stat_ref):
    chunk = 2 * LANES
    scale = jnp.concatenate([scale_ref[r : r + 1, :] for r in range(scale_ref.shape[0])], axis=1)
    for c in range(got_ref.shape[0] // chunk):
        at = slice(c * chunk, (c + 1) * chunk)
        std_ref[at, :] = (got_ref[at, :].astype(jnp.float32) * scale).astype(jnp.bfloat16)
    block_stats(block_ref[...], std_ref, stat_ref)


def combine(stats_ref, same_ref, swap_ref, slab_rows):
    peers, rows, lanes = stats_ref.shape
    own = stats_ref[...].reshape(peers * rows, lanes)
    lane = lax.broadcasted_iota(jnp.int32, own.shape, 1)
    ahead = pltpu.roll(own, lanes - slab_rows, 1)
    behind = pltpu.roll(own, slab_rows, 1)
    other = jnp.where(lane % (2 * slab_rows) < slab_rows, ahead, behind)
    own = own.reshape(peers, rows, lanes)
    other = other.reshape(peers, rows, lanes)
    first = jnp.where(same_ref[...] > 0, own, -jnp.inf)
    second = jnp.where(swap_ref[...] > 0, other, -jnp.inf)
    summit = jnp.max(jnp.maximum(first, second), axis=0)
    live = summit > -jnp.inf
    summit = jnp.where(live, summit, 0.0)
    total = jnp.sum(jnp.exp(first - summit) + jnp.exp(second - summit), axis=0)
    return jnp.where(live, summit + jnp.log(jnp.where(live, total, 1.0)), jnp.inf)


def update(normal, logits, std_ref, old):
    parts = []
    for c, chunk, values in logits:
        for h in range(0, chunk, LANES):
            r = (c + h) // LANES
            parts.append(jnp.exp(values[:, h : h + LANES] - normal[r : r + 1, :]))
    resp = jnp.concatenate(parts, axis=1)
    weight = jnp.sum(resp, axis=1, keepdims=True)
    sums = lax.dot_general(
        resp.astype(jnp.bfloat16),
        std_ref[...],
        (((1,), (0,)), ((), ())),
        preferred_element_type=jnp.float32,
    )
    return (sums + old) / (weight + prior_count), weight


def middle_body(
    slab_rows,
    stats_ref,
    same_ref,
    swap_ref,
    std_ref,
    old_ref,
    new_ref,
    next_ref,
    stat_ref,
):
    normal = combine(stats_ref, same_ref, swap_ref, slab_rows)
    old = old_ref[...]
    logits = block_logits(old.astype(jnp.bfloat16), std_ref)
    current, _ = update(normal, logits, std_ref, old.astype(jnp.float32))
    new_ref[...] = current
    block_stats(current.astype(jnp.bfloat16), std_ref, stat_ref, next_ref)


def last_body(
    slab_rows, stats_ref, same_ref, swap_ref, logits_ref, std_ref, old_ref, new_ref, weight_ref
):
    normal = combine(stats_ref, same_ref, swap_ref, slab_rows)
    logits = [(0, logits_ref.shape[1], logits_ref[...])]
    current, weight = update(normal, logits, std_ref, old_ref[...])
    new_ref[...] = current
    flat = jnp.transpose(jnp.broadcast_to(weight, (weight.shape[0], LANES)))
    weight_ref[...] = flat[:1, :]


def spread(x):
    return lax.all_to_all(x, DP, split_axis=0, concat_axis=0, tiled=True)


def per_device(embeddings, coarse_lists, home, centroids):
    row_count, width = embeddings.shape
    peers = lax.axis_size(DP)
    total_rows = row_count * peers * lax.axis_size(("y", "x"))
    slabs, listed = coarse_lists.shape
    slab_rows = row_count // slabs
    most = 2
    slots = peers * most * slab_rows
    f32 = jnp.float32

    with jax.named_scope("sums_and_lists"):
        lists = coarse_lists.T
        payload = pl.pallas_call(
            share_body,
            out_shape=jax.ShapeDtypeStruct((peers, width // LANES + 1, LANES), f32),
            in_specs=[pl.BlockSpec(memory_space=pltpu.SMEM)] + vmem(1),
            out_specs=vmem(1)[0],
        )(lists, embeddings)
        shared = spread(payload)

    with jax.named_scope("slabs_out"):
        outgoing = pl.pallas_call(
            lambda *refs: dispatch(slab_rows, most, peers, *refs),
            out_shape=jax.ShapeDtypeStruct((slots, width), jnp.bfloat16),
            in_specs=[pl.BlockSpec(memory_space=pltpu.SMEM)] * 2 + vmem(1),
            out_specs=vmem(1)[0],
            scratch_shapes=[pltpu.SMEM((peers * (most + 1),), jnp.int32)],
        )(lists, home, embeddings)
        received = spread(outgoing.reshape(peers, most * slab_rows, width)).reshape(slots, width)

    with jax.named_scope("feature_scale"):
        total = jnp.sum(shared[:, : width // LANES], axis=0)
        total = lax.psum(lax.psum(total, "x"), "y")
        scale = lax.rsqrt(total / total_rows + 1e-06)

    with jax.named_scope("slot_masks"):
        me = lax.axis_index(DP)
        ids = jnp.arange(peers, dtype=jnp.int32)
        lists_all = shared[:, width // LANES, : slabs * listed].astype(jnp.int32)
        home_of = jnp.sum(jnp.where(lists_all[:, :, None] == ids, home[0], 0), axis=2)
        hits = jnp.any(home_of.reshape(peers, slabs, listed)[..., None] == ids, axis=2)
        order = jnp.arange(slabs)
        earlier = (order[None, :] < order[:, None])[None, :, :, None]
        before = jnp.sum(jnp.where(earlier & hits[:, None], 1, 0), axis=2)
        place = jnp.where(hits, before, -1)
        mine = jnp.sum(jnp.where(ids == me, place, 0), axis=2)
        turn = jnp.arange(most)
        chosen = mine[:, None, :] == turn[:, None]

        def lanes_of(wanted):
            found = chosen[..., None] & (place[:, None] == wanted[:, None, None])
            found = jnp.any(found, axis=2).astype(f32)
            found = found.transpose(2, 0, 1).reshape(peers, peers * most)
            found = jnp.repeat(found, slab_rows, axis=1).reshape(peers, -1, LANES)
            return jnp.pad(found, ((0, 0), (0, -found.shape[1] % 8), (0, 0)))

        same, swap = lanes_of(turn), lanes_of(1 - turn)

    block = centroids[0, 0]
    rows_of_stat = same.shape[1]
    work = 2 * slots * block.shape[0] * width
    logits_shape = jax.ShapeDtypeStruct((block.shape[0], slots), f32)
    stat_shape = jax.ShapeDtypeStruct((peers, rows_of_stat, LANES), f32)
    block_shape = jax.ShapeDtypeStruct(block.shape, f32)
    with jax.named_scope("first_logits"):
        std, stat = call(
            first_body,
            (jax.ShapeDtypeStruct((slots, width), jnp.bfloat16), stat_shape),
            vmem(5),
            work,
            4 << 20,
        )(received, scale, block, same, swap)
    old = block
    for turn_index in range(ITERS - 1):
        with jax.named_scope("stats_out"):
            stats = spread(stat)
        with jax.named_scope("middle_update"):
            old, logits, stat = call(
                lambda *refs: middle_body(slab_rows, *refs),
                (block_shape, logits_shape, stat_shape),
                vmem(5),
                3 * work,
                5 << 20,
            )(stats, same, swap, std, old)
    with jax.named_scope("last_stats_out"):
        stats = spread(stat)
    with jax.named_scope("last_update"):
        current, weight = call(
            lambda *refs: last_body(slab_rows, *refs),
            (block_shape, jax.ShapeDtypeStruct((1, block.shape[0]), f32)),
            vmem(6),
            work,
            5 << 20,
        )(stats, same, swap, logits, std, old)
    return current[None, None], weight[None]


def solution(mesh):
    chips, rows = 12, 8
    grid = np.asarray(mesh.devices).reshape(chips, mesh.devices.shape[0] // chips, rows, -1)
    fine = Mesh(grid, ("z", "core", "y", "x"))
    group = ("y", "x")
    return jax.shard_map(
        per_device,
        mesh=fine,
        in_specs=(P(DP + group, None), P(DP + group, None), P(group, None), P(group, DP, None, None)),
        out_specs=(P(group, DP, None, None), P(group, DP, None)),
        check_vma=False,
    )
```

```python
import math

import jax
import jax.numpy as jnp
import numpy as np
from jax import lax
from jax.experimental import pallas as pl
from jax.experimental.pallas import tpu as pltpu
from jax.sharding import Mesh, PartitionSpec as P

ITERS = 2
DP = ("z", "core")
LANES = 128

prior_count = 1.0


def vmem(count):
    return [pl.BlockSpec(memory_space=pltpu.VMEM)] * count


def call(body, outs, specs, flops, moved):
    return pl.pallas_call(
        body,
        out_shape=outs,
        in_specs=specs,
        out_specs=tuple(vmem(len(outs))),
        compiler_params=pltpu.CompilerParams(vmem_limit_bytes=16 * 2**20),
        cost_estimate=pl.CostEstimate(flops=flops, bytes_accessed=moved, transcendentals=0),
    )


def share_body(lists_ref, emb_ref, out_ref):
    listed, slabs = lists_ref.shape
    wide = emb_ref[...].astype(jnp.float32)
    squares = jnp.sum(wide * wide, axis=0, keepdims=True)
    lane = lax.broadcasted_iota(jnp.int32, (1, LANES), 1)
    names = jnp.zeros((1, LANES), jnp.int32)
    for n in range(slabs * listed):
        names = jnp.where(lane == n, lists_ref[n % listed, n // listed], names)
    half = wide.shape[1] // 2
    upper = jnp.concatenate([squares[:, :half], names.astype(jnp.float32)], axis=1)
    lower = jnp.concatenate([squares[:, half:], jnp.zeros((1, LANES), jnp.float32)], axis=1)
    payload = jnp.concatenate([upper, lower], axis=0).astype(jnp.bfloat16)
    for p in range(out_ref.shape[0]):
        out_ref[p] = payload


def dispatch(slab_rows, most, peers, lists_ref, home_ref, emb_ref, out_ref, table):
    listed, slabs = lists_ref.shape

    def clear(p, carry):
        table[p] = 0
        return carry

    lax.fori_loop(0, peers * most, clear, 0)

    def count_clear(p, carry):
        table[peers * most + p] = 0
        return carry

    lax.fori_loop(0, peers, count_clear, 0)

    def place(n, carry):
        slab, k = n // listed, n % listed
        p = home_ref[0, lists_ref[k, slab]]
        seen = table[peers * most + p]
        table[p * most + jnp.minimum(seen, most - 1)] = slab
        table[peers * most + p] = seen + 1
        return carry

    lax.fori_loop(0, slabs * listed, place, 0)

    def copy(n, carry):
        source = pl.multiple_of(table[n] * slab_rows, slab_rows)
        target = pl.multiple_of(n * slab_rows, slab_rows)
        out_ref[pl.ds(target, slab_rows), :] = emb_ref[pl.ds(source, slab_rows), :]
        return carry

    lax.fori_loop(0, peers * most, copy, 0)


def block_logits(block_low, std_ref):
    width = block_low.shape[1]
    wide = block_low.astype(jnp.float32)
    cnorm = jnp.sum(wide * wide, axis=1, keepdims=True)
    chunk = 2 * LANES
    for c in range(0, std_ref.shape[0], chunk):
        products = lax.dot_general(
            block_low,
            std_ref[c : c + chunk, :],
            (((1,), (1,)), ((), ())),
            preferred_element_type=jnp.float32,
        )
        yield c, chunk, (2.0 * products - cnorm) * (1.0 / math.sqrt(width))


def block_stats(block_low, std_ref, stat_ref, logits_ref=None):
    lines = []
    for c, chunk, logits in block_logits(block_low, std_ref):
        if logits_ref is not None:
            logits_ref[:, c : c + chunk] = logits
        largest = jnp.max(logits, axis=0, keepdims=True)
        total = jnp.sum(jnp.exp(logits - largest), axis=0, keepdims=True)
        lines.append(largest + jnp.log(total))
    stat = jnp.concatenate(lines, axis=1)
    for p in range(stat_ref.shape[0]):
        stat_ref[p] = stat


def first_body(got_ref, scale_ref, block_ref, same_ref, swap_ref, std_ref, stat_ref):
    chunk = 2 * LANES
    scale = jnp.concatenate([scale_ref[r : r + 1, :] for r in range(scale_ref.shape[0])], axis=1)
    for c in range(got_ref.shape[0] // chunk):
        at = slice(c * chunk, (c + 1) * chunk)
        std_ref[at, :] = (got_ref[at, :].astype(jnp.float32) * scale).astype(jnp.bfloat16)
    block_stats(block_ref[...], std_ref, stat_ref)


def combine(stats_ref, same_ref, swap_ref, slab_rows):
    lines = []
    for c in range(0, stats_ref.shape[2], LANES):
        own = stats_ref[:, 0, c : c + LANES]
        lane = lax.broadcasted_iota(jnp.int32, own.shape, 1)
        ahead = pltpu.roll(own, LANES - slab_rows, 1)
        behind = pltpu.roll(own, slab_rows, 1)
        other = jnp.where(lane % (2 * slab_rows) < slab_rows, ahead, behind)
        first = jnp.where(same_ref[:, c : c + LANES] > 0, own, -jnp.inf)
        second = jnp.where(swap_ref[:, c : c + LANES] > 0, other, -jnp.inf)
        summit = jnp.max(jnp.maximum(first, second), axis=0, keepdims=True)
        live = summit > -jnp.inf
        summit = jnp.where(live, summit, 0.0)
        total = jnp.sum(jnp.exp(first - summit) + jnp.exp(second - summit), axis=0, keepdims=True)
        lines.append(jnp.where(live, summit + jnp.log(jnp.where(live, total, 1.0)), jnp.inf))
    return jnp.concatenate(lines, axis=1)


def update(normal, logits, std_ref, old):
    parts = []
    for c, chunk, values in logits:
        parts.append(jnp.exp(values - normal[:, c : c + chunk]))
    resp = jnp.concatenate(parts, axis=1)
    weight = jnp.sum(resp, axis=1, keepdims=True)
    sums = lax.dot_general(
        resp.astype(jnp.bfloat16),
        std_ref[...],
        (((1,), (0,)), ((), ())),
        preferred_element_type=jnp.float32,
    )
    return (sums + old) / (weight + prior_count), weight


def middle_body(
    slab_rows,
    stats_ref,
    same_ref,
    swap_ref,
    std_ref,
    old_ref,
    new_ref,
    next_ref,
    stat_ref,
):
    normal = combine(stats_ref, same_ref, swap_ref, slab_rows)
    old = old_ref[...]
    logits = block_logits(old.astype(jnp.bfloat16), std_ref)
    current, _ = update(normal, logits, std_ref, old.astype(jnp.float32))
    new_ref[...] = current
    block_stats(current.astype(jnp.bfloat16), std_ref, stat_ref, next_ref)


def last_body(
    slab_rows, stats_ref, same_ref, swap_ref, logits_ref, std_ref, old_ref, new_ref, weight_ref
):
    normal = combine(stats_ref, same_ref, swap_ref, slab_rows)
    logits = [(0, logits_ref.shape[1], logits_ref[...])]
    current, weight = update(normal, logits, std_ref, old_ref[...])
    new_ref[...] = current
    flat = jnp.transpose(jnp.broadcast_to(weight, (weight.shape[0], LANES)))
    weight_ref[...] = flat[:1, :]


def spread(x):
    return lax.all_to_all(x, DP, split_axis=0, concat_axis=0, tiled=True)


def per_device(embeddings, coarse_lists, home, centroids):
    row_count, width = embeddings.shape
    peers = lax.axis_size(DP)
    total_rows = row_count * peers * lax.axis_size(("y", "x"))
    slabs, listed = coarse_lists.shape
    slab_rows = row_count // slabs
    most = 2
    slots = peers * most * slab_rows
    f32 = jnp.float32

    with jax.named_scope("sums_and_lists"):
        lists = coarse_lists.T
        payload = pl.pallas_call(
            share_body,
            out_shape=jax.ShapeDtypeStruct((peers, 2, width // 2 + LANES), jnp.bfloat16),
            in_specs=[pl.BlockSpec(memory_space=pltpu.SMEM)] + vmem(1),
            out_specs=vmem(1)[0],
        )(lists, embeddings)
        shared = spread(payload)

    with jax.named_scope("slabs_out"):
        outgoing = pl.pallas_call(
            lambda *refs: dispatch(slab_rows, most, peers, *refs),
            out_shape=jax.ShapeDtypeStruct((slots, width), jnp.bfloat16),
            in_specs=[pl.BlockSpec(memory_space=pltpu.SMEM)] * 2 + vmem(1),
            out_specs=vmem(1)[0],
            scratch_shapes=[pltpu.SMEM((peers * (most + 1),), jnp.int32)],
        )(lists, home, embeddings)
        received = spread(outgoing.reshape(peers, most * slab_rows, width)).reshape(slots, width)

    with jax.named_scope("feature_scale"):
        total = jnp.sum(shared[:, :, : width // 2].astype(f32), axis=0).reshape(-1, LANES)
        total = lax.psum(lax.psum(total, "x"), "y")
        scale = lax.rsqrt(total / total_rows + 1e-06)

    with jax.named_scope("slot_masks"):
        me = lax.axis_index(DP)
        ids = jnp.arange(peers, dtype=jnp.int32)
        lists_all = shared[:, 0, width // 2 : width // 2 + slabs * listed].astype(jnp.int32)
        home_of = jnp.sum(jnp.where(lists_all[:, :, None] == ids, home[0], 0), axis=2)
        hits = jnp.any(home_of.reshape(peers, slabs, listed)[..., None] == ids, axis=2)
        order = jnp.arange(slabs)
        earlier = (order[None, :] < order[:, None])[None, :, :, None]
        before = jnp.sum(jnp.where(earlier & hits[:, None], 1, 0), axis=2)
        place = jnp.where(hits, before, -1)
        mine = jnp.sum(jnp.where(ids == me, place, 0), axis=2)
        turn = jnp.arange(most)
        chosen = mine[:, None, :] == turn[:, None]

        def lanes_of(wanted):
            found = chosen[..., None] & (place[:, None] == wanted[:, None, None])
            found = jnp.any(found, axis=2).astype(f32)
            found = found.transpose(2, 0, 1).reshape(peers, peers * most)
            return jnp.repeat(found, slab_rows, axis=1)

        same, swap = lanes_of(turn), lanes_of(1 - turn)

    block = centroids[0, 0]
    work = 2 * slots * block.shape[0] * width
    logits_shape = jax.ShapeDtypeStruct((block.shape[0], slots), f32)
    stat_shape = jax.ShapeDtypeStruct((peers, 1, slots), f32)
    block_shape = jax.ShapeDtypeStruct(block.shape, f32)
    with jax.named_scope("first_logits"):
        std, stat = call(
            first_body,
            (jax.ShapeDtypeStruct((slots, width), jnp.bfloat16), stat_shape),
            vmem(5),
            work,
            4 << 20,
        )(received, scale, block, same, swap)
    old = block
    for turn_index in range(ITERS - 1):
        with jax.named_scope("stats_out"):
            stats = spread(stat)
        with jax.named_scope("middle_update"):
            old, logits, stat = call(
                lambda *refs: middle_body(slab_rows, *refs),
                (block_shape, logits_shape, stat_shape),
                vmem(5),
                3 * work,
                5 << 20,
            )(stats, same, swap, std, old)
    with jax.named_scope("last_stats_out"):
        stats = spread(stat)
    with jax.named_scope("last_update"):
        current, weight = call(
            lambda *refs: last_body(slab_rows, *refs),
            (block_shape, jax.ShapeDtypeStruct((1, block.shape[0]), f32)),
            vmem(6),
            work,
            5 << 20,
        )(stats, same, swap, logits, std, old)
    return current[None, None], weight[None]


def solution(mesh):
    chips, rows = 12, 8
    grid = np.asarray(mesh.devices).reshape(chips, mesh.devices.shape[0] // chips, rows, -1)
    fine = Mesh(grid, ("z", "core", "y", "x"))
    group = ("y", "x")
    return jax.shard_map(
        per_device,
        mesh=fine,
        in_specs=(P(DP + group, None), P(DP + group, None), P(group, None), P(group, DP, None, None)),
        out_specs=(P(group, DP, None, None), P(group, DP, None)),
        check_vma=False,
    )
```

```python
import math

import jax
import jax.numpy as jnp
import numpy as np
from jax import lax
from jax.experimental import pallas as pl
from jax.experimental.pallas import tpu as pltpu
from jax.sharding import Mesh, PartitionSpec as P

ITERS = 2
DP = ("z", "core")
LANES = 128

prior_count = 1.0


def vmem(count):
    return [pl.BlockSpec(memory_space=pltpu.VMEM)] * count


def call(body, outs, specs, flops, moved):
    return pl.pallas_call(
        body,
        out_shape=outs,
        in_specs=specs,
        out_specs=tuple(vmem(len(outs))),
        compiler_params=pltpu.CompilerParams(vmem_limit_bytes=16 * 2**20),
        cost_estimate=pl.CostEstimate(flops=flops, bytes_accessed=moved, transcendentals=0),
    )


def share_body(cores, lists_ref, emb_ref, out_ref):
    listed, slabs = lists_ref.shape
    wide = emb_ref[...].astype(jnp.float32)
    squares = jnp.sum(wide * wide, axis=0, keepdims=True)
    lane = lax.broadcasted_iota(jnp.int32, (1, LANES), 1)
    names = jnp.zeros((1, LANES), jnp.int32)
    for n in range(slabs * listed):
        names = jnp.where(lane == n, lists_ref[n % listed, n // listed], names)
    part = wide.shape[1] // (2 * cores)
    names = names.astype(jnp.float32)
    for core in range(cores):
        at = 2 * part * core
        upper = jnp.concatenate([squares[:, at : at + part], names], axis=1)
        lower = jnp.concatenate([squares[:, at + part : at + 2 * part], names], axis=1)
        payload = jnp.concatenate([upper, lower], axis=0).astype(jnp.bfloat16)
        for p in range(core, out_ref.shape[0], cores):
            out_ref[p] = payload


def dispatch(slab_rows, most, peers, lists_ref, home_ref, emb_ref, out_ref, table):
    listed, slabs = lists_ref.shape

    def clear(p, carry):
        table[p] = 0
        return carry

    lax.fori_loop(0, peers * most, clear, 0)

    def count_clear(p, carry):
        table[peers * most + p] = 0
        return carry

    lax.fori_loop(0, peers, count_clear, 0)

    def place(n, carry):
        slab, k = n // listed, n % listed
        p = home_ref[0, lists_ref[k, slab]]
        seen = table[peers * most + p]
        table[p * most + jnp.minimum(seen, most - 1)] = slab
        table[peers * most + p] = seen + 1
        return carry

    lax.fori_loop(0, slabs * listed, place, 0)

    def copy(n, carry):
        source = pl.multiple_of(table[n] * slab_rows, slab_rows)
        target = pl.multiple_of(n * slab_rows, slab_rows)
        out_ref[pl.ds(target, slab_rows), :] = emb_ref[pl.ds(source, slab_rows), :]
        return carry

    lax.fori_loop(0, peers * most, copy, 0)


def block_logits(block_low, std_ref):
    width = block_low.shape[1]
    wide = block_low.astype(jnp.float32)
    cnorm = jnp.sum(wide * wide, axis=1, keepdims=True)
    chunk = 2 * LANES
    for c in range(0, std_ref.shape[0], chunk):
        products = lax.dot_general(
            block_low,
            std_ref[c : c + chunk, :],
            (((1,), (1,)), ((), ())),
            preferred_element_type=jnp.float32,
        )
        yield c, chunk, (2.0 * products - cnorm) * (1.0 / math.sqrt(width))


def block_stats(block_low, std_ref, stat_ref, logits_ref=None):
    lines = []
    for c, chunk, logits in block_logits(block_low, std_ref):
        if logits_ref is not None:
            logits_ref[:, c : c + chunk] = logits
        largest = jnp.max(logits, axis=0, keepdims=True)
        total = jnp.sum(jnp.exp(logits - largest), axis=0, keepdims=True)
        lines.append(largest + jnp.log(total))
    stat = jnp.concatenate(lines, axis=1)
    for p in range(stat_ref.shape[0]):
        stat_ref[p] = stat


def first_body(
    got_ref, scale_ref, block_ref, same_ref, swap_ref, std_ref, logits_ref, stat_ref
):
    chunk = 2 * LANES
    scale = jnp.concatenate([scale_ref[r : r + 1, :] for r in range(scale_ref.shape[0])], axis=1)
    for c in range(got_ref.shape[0] // chunk):
        at = slice(c * chunk, (c + 1) * chunk)
        std_ref[at, :] = (got_ref[at, :].astype(jnp.float32) * scale).astype(jnp.bfloat16)
    block_stats(block_ref[...], std_ref, stat_ref, logits_ref)


def combine(stats_ref, same_ref, swap_ref, slab_rows):
    lines = []
    for c in range(0, stats_ref.shape[2], LANES):
        own = stats_ref[:, 0, c : c + LANES]
        lane = lax.broadcasted_iota(jnp.int32, own.shape, 1)
        ahead = pltpu.roll(own, LANES - slab_rows, 1)
        behind = pltpu.roll(own, slab_rows, 1)
        other = jnp.where(lane % (2 * slab_rows) < slab_rows, ahead, behind)
        first = jnp.where(same_ref[:, c : c + LANES] > 0, own, -jnp.inf)
        second = jnp.where(swap_ref[:, c : c + LANES] > 0, other, -jnp.inf)
        summit = jnp.max(jnp.maximum(first, second), axis=0, keepdims=True)
        live = summit > -jnp.inf
        summit = jnp.where(live, summit, 0.0)
        total = jnp.sum(jnp.exp(first - summit) + jnp.exp(second - summit), axis=0, keepdims=True)
        lines.append(jnp.where(live, summit + jnp.log(jnp.where(live, total, 1.0)), jnp.inf))
    return jnp.concatenate(lines, axis=1)


def update(normal, logits, std_ref, old):
    parts = []
    for c, chunk, values in logits:
        parts.append(jnp.exp(values - normal[:, c : c + chunk]))
    resp = jnp.concatenate(parts, axis=1)
    weight = jnp.sum(resp, axis=1, keepdims=True)
    sums = lax.dot_general(
        resp.astype(jnp.bfloat16),
        std_ref[...],
        (((1,), (0,)), ((), ())),
        preferred_element_type=jnp.float32,
    )
    return (sums + old) / (weight + prior_count), weight


def middle_body(
    slab_rows,
    stats_ref,
    same_ref,
    swap_ref,
    logits_ref,
    std_ref,
    old_ref,
    new_ref,
    next_ref,
    stat_ref,
):
    normal = combine(stats_ref, same_ref, swap_ref, slab_rows)
    old = old_ref[...]
    logits = [(0, logits_ref.shape[1], logits_ref[...])]
    current, _ = update(normal, logits, std_ref, old.astype(jnp.float32))
    new_ref[...] = current
    block_stats(current.astype(jnp.bfloat16), std_ref, stat_ref, next_ref)


def last_body(
    slab_rows, stats_ref, same_ref, swap_ref, logits_ref, std_ref, old_ref, new_ref, weight_ref
):
    normal = combine(stats_ref, same_ref, swap_ref, slab_rows)
    logits = [(0, logits_ref.shape[1], logits_ref[...])]
    current, weight = update(normal, logits, std_ref, old_ref[...])
    new_ref[...] = current
    flat = jnp.transpose(jnp.broadcast_to(weight, (weight.shape[0], LANES)))
    weight_ref[...] = flat[:1, :]


def spread(x):
    return lax.all_to_all(x, DP, split_axis=0, concat_axis=0, tiled=True)


def per_device(embeddings, coarse_lists, home, centroids):
    row_count, width = embeddings.shape
    peers = lax.axis_size(DP)
    total_rows = row_count * peers * lax.axis_size(("y", "x"))
    slabs, listed = coarse_lists.shape
    slab_rows = row_count // slabs
    most = 2
    cores = lax.axis_size(DP[1])
    part = width // (2 * cores)
    slots = peers * most * slab_rows
    f32 = jnp.float32

    with jax.named_scope("sums_and_lists"):
        lists = coarse_lists.T
        payload = pl.pallas_call(
            lambda *refs: share_body(cores, *refs),
            out_shape=jax.ShapeDtypeStruct((peers, 2, part + LANES), jnp.bfloat16),
            in_specs=[pl.BlockSpec(memory_space=pltpu.SMEM)] + vmem(1),
            out_specs=vmem(1)[0],
        )(lists, embeddings)
        shared = spread(payload)

    with jax.named_scope("slabs_out"):
        outgoing = pl.pallas_call(
            lambda *refs: dispatch(slab_rows, most, peers, *refs),
            out_shape=jax.ShapeDtypeStruct((slots, width), jnp.bfloat16),
            in_specs=[pl.BlockSpec(memory_space=pltpu.SMEM)] * 2 + vmem(1),
            out_specs=vmem(1)[0],
            scratch_shapes=[pltpu.SMEM((peers * (most + 1),), jnp.int32)],
        )(lists, home, embeddings)
        received = spread(outgoing.reshape(peers, most * slab_rows, width)).reshape(slots, width)

    with jax.named_scope("feature_scale"):
        total = jnp.sum(shared[:, :, :part].astype(f32), axis=0).reshape(-1, LANES)
        total = lax.psum(lax.psum(total, "x"), "y")
        total = lax.all_gather(total, DP[1], tiled=True)
        scale = lax.rsqrt(total / total_rows + 1e-06)

    with jax.named_scope("slot_masks"):
        me = lax.axis_index(DP)
        ids = jnp.arange(peers, dtype=jnp.int32)
        lists_all = shared[:, 0, part : part + slabs * listed].astype(jnp.int32)
        home_of = jnp.sum(jnp.where(lists_all[:, :, None] == ids, home[0], 0), axis=2)
        hits = jnp.any(home_of.reshape(peers, slabs, listed)[..., None] == ids, axis=2)
        order = jnp.arange(slabs)
        earlier = (order[None, :] < order[:, None])[None, :, :, None]
        before = jnp.sum(jnp.where(earlier & hits[:, None], 1, 0), axis=2)
        place = jnp.where(hits, before, -1)
        mine = jnp.sum(jnp.where(ids == me, place, 0), axis=2)
        turn = jnp.arange(most)
        chosen = mine[:, None, :] == turn[:, None]

        def lanes_of(wanted):
            found = chosen[..., None] & (place[:, None] == wanted[:, None, None])
            found = jnp.any(found, axis=2).astype(f32)
            found = found.transpose(2, 0, 1).reshape(peers, peers * most)
            return jnp.repeat(found, slab_rows, axis=1)

        same, swap = lanes_of(turn), lanes_of(1 - turn)

    block = centroids[0, 0]
    work = 2 * slots * block.shape[0] * width
    logits_shape = jax.ShapeDtypeStruct((block.shape[0], slots), f32)
    stat_shape = jax.ShapeDtypeStruct((peers, 1, slots), f32)
    block_shape = jax.ShapeDtypeStruct(block.shape, f32)
    with jax.named_scope("first_logits"):
        std, logits, stat = call(
            first_body,
            (jax.ShapeDtypeStruct((slots, width), jnp.bfloat16), logits_shape, stat_shape),
            vmem(5),
            work,
            4 << 20,
        )(received, scale, block, same, swap)
    old = block
    for turn_index in range(ITERS - 1):
        with jax.named_scope("stats_out"):
            stats = spread(stat)
        with jax.named_scope("middle_update"):
            old, logits, stat = call(
                lambda *refs: middle_body(slab_rows, *refs),
                (block_shape, logits_shape, stat_shape),
                vmem(6),
                2 * work,
                5 << 20,
            )(stats, same, swap, logits, std, old)
    with jax.named_scope("last_stats_out"):
        stats = spread(stat)
    with jax.named_scope("last_update"):
        current, weight = call(
            lambda *refs: last_body(slab_rows, *refs),
            (block_shape, jax.ShapeDtypeStruct((1, block.shape[0]), f32)),
            vmem(6),
            work,
            5 << 20,
        )(stats, same, swap, logits, std, old)
    return current[None, None], weight[None]


def solution(mesh):
    chips, rows = 12, 8
    grid = np.asarray(mesh.devices).reshape(chips, mesh.devices.shape[0] // chips, rows, -1)
    fine = Mesh(grid, ("z", "core", "y", "x"))
    group = ("y", "x")
    return jax.shard_map(
        per_device,
        mesh=fine,
        in_specs=(P(DP + group, None), P(DP + group, None), P(group, None), P(group, DP, None, None)),
        out_specs=(P(group, DP, None, None), P(group, DP, None)),
        check_vma=False,
    )
```

```python
import math

import jax
import jax.numpy as jnp
import numpy as np
from jax import lax
from jax.experimental import pallas as pl
from jax.experimental.pallas import tpu as pltpu
from jax.sharding import Mesh, PartitionSpec as P

ITERS = 2
DP = ("high", "low", "core")
PEERS = ("low", "core", "high")
LOW = 4
LANES = 128

prior_count = 1.0


def vmem(count):
    return [pl.BlockSpec(memory_space=pltpu.VMEM)] * count


def call(body, outs, specs, flops, moved):
    return pl.pallas_call(
        body,
        out_shape=outs,
        in_specs=specs,
        out_specs=tuple(vmem(len(outs))),
        compiler_params=pltpu.CompilerParams(vmem_limit_bytes=16 * 2**20),
        cost_estimate=pl.CostEstimate(flops=flops, bytes_accessed=moved, transcendentals=0),
    )


def peer_of(position, peers, cores):
    high = peers // (cores * LOW)
    chip, core = position // cores, position % cores
    return (chip % LOW * cores + core) * high + chip // LOW


def share_body(cores, lists_ref, emb_ref, out_ref):
    listed, slabs = lists_ref.shape
    wide = emb_ref[...].astype(jnp.float32)
    squares = jnp.sum(wide * wide, axis=0, keepdims=True)
    lane = lax.broadcasted_iota(jnp.int32, (1, LANES), 1)
    names = jnp.zeros((1, LANES), jnp.int32)
    for n in range(slabs * listed):
        names = jnp.where(lane == n, lists_ref[n % listed, n // listed], names)
    part = wide.shape[1] // (2 * cores)
    names = names.astype(jnp.float32)
    for core in range(cores):
        at = 2 * part * core
        upper = jnp.concatenate([squares[:, at : at + part], names], axis=1)
        lower = jnp.concatenate([squares[:, at + part : at + 2 * part], names], axis=1)
        payload = jnp.concatenate([upper, lower], axis=0).astype(jnp.bfloat16)
        for position in range(core, out_ref.shape[0], cores):
            out_ref[peer_of(position, out_ref.shape[0], cores)] = payload


def dispatch(slab_rows, most, peers, cores, lists_ref, home_ref, emb_ref, out_ref, table):
    listed, slabs = lists_ref.shape

    def clear(p, carry):
        table[p] = 0
        return carry

    lax.fori_loop(0, peers * most, clear, 0)

    def count_clear(p, carry):
        table[peers * most + p] = 0
        return carry

    lax.fori_loop(0, peers, count_clear, 0)

    def place(n, carry):
        slab, k = n // listed, n % listed
        p = peer_of(home_ref[0, lists_ref[k, slab]], peers, cores)
        seen = table[peers * most + p]
        table[p * most + jnp.minimum(seen, most - 1)] = slab
        table[peers * most + p] = seen + 1
        return carry

    lax.fori_loop(0, slabs * listed, place, 0)

    def copy(n, carry):
        source = pl.multiple_of(table[n] * slab_rows, slab_rows)
        target = pl.multiple_of(n * slab_rows, slab_rows)
        out_ref[pl.ds(target, slab_rows), :] = emb_ref[pl.ds(source, slab_rows), :]
        return carry

    lax.fori_loop(0, peers * most, copy, 0)


def block_logits(block_low, std_ref):
    width = block_low.shape[1]
    wide = block_low.astype(jnp.float32)
    cnorm = jnp.sum(wide * wide, axis=1, keepdims=True)
    chunk = 2 * LANES
    for c in range(0, std_ref.shape[0], chunk):
        products = lax.dot_general(
            block_low,
            std_ref[c : c + chunk, :],
            (((1,), (1,)), ((), ())),
            preferred_element_type=jnp.float32,
        )
        yield c, chunk, (2.0 * products - cnorm) * (1.0 / math.sqrt(width))


def block_stats(block_low, std_ref, stat_ref, logits_ref=None):
    lines = []
    for c, chunk, logits in block_logits(block_low, std_ref):
        if logits_ref is not None:
            logits_ref[:, c : c + chunk] = logits
        largest = jnp.max(logits, axis=0, keepdims=True)
        total = jnp.sum(jnp.exp(logits - largest), axis=0, keepdims=True)
        lines.append(largest + jnp.log(total))
    stat = jnp.concatenate(lines, axis=1)
    for p in range(stat_ref.shape[0]):
        stat_ref[p] = stat


def first_body(
    got_ref, scale_ref, block_ref, same_ref, swap_ref, std_ref, logits_ref, stat_ref
):
    chunk = 2 * LANES
    scale = jnp.concatenate([scale_ref[r : r + 1, :] for r in range(scale_ref.shape[0])], axis=1)
    for c in range(got_ref.shape[0] // chunk):
        at = slice(c * chunk, (c + 1) * chunk)
        std_ref[at, :] = (got_ref[at, :].astype(jnp.float32) * scale).astype(jnp.bfloat16)
    block_stats(block_ref[...], std_ref, stat_ref, logits_ref)


def combine(stats_ref, same_ref, swap_ref, slab_rows):
    lines = []
    for c in range(0, stats_ref.shape[2], LANES):
        own = stats_ref[:, 0, c : c + LANES]
        lane = lax.broadcasted_iota(jnp.int32, own.shape, 1)
        ahead = pltpu.roll(own, LANES - slab_rows, 1)
        behind = pltpu.roll(own, slab_rows, 1)
        other = jnp.where(lane % (2 * slab_rows) < slab_rows, ahead, behind)
        first = jnp.where(same_ref[:, c : c + LANES] > 0, own, -jnp.inf)
        second = jnp.where(swap_ref[:, c : c + LANES] > 0, other, -jnp.inf)
        summit = jnp.max(jnp.maximum(first, second), axis=0, keepdims=True)
        live = summit > -jnp.inf
        summit = jnp.where(live, summit, 0.0)
        total = jnp.sum(jnp.exp(first - summit) + jnp.exp(second - summit), axis=0, keepdims=True)
        lines.append(jnp.where(live, summit + jnp.log(jnp.where(live, total, 1.0)), jnp.inf))
    return jnp.concatenate(lines, axis=1)


def update(normal, logits, std_ref, old):
    parts = []
    for c, chunk, values in logits:
        parts.append(jnp.exp(values - normal[:, c : c + chunk]))
    resp = jnp.concatenate(parts, axis=1)
    weight = jnp.sum(resp, axis=1, keepdims=True)
    sums = lax.dot_general(
        resp.astype(jnp.bfloat16),
        std_ref[...],
        (((1,), (0,)), ((), ())),
        preferred_element_type=jnp.float32,
    )
    return (sums + old) / (weight + prior_count), weight


def middle_body(
    slab_rows,
    stats_ref,
    same_ref,
    swap_ref,
    logits_ref,
    std_ref,
    old_ref,
    new_ref,
    next_ref,
    stat_ref,
):
    normal = combine(stats_ref, same_ref, swap_ref, slab_rows)
    old = old_ref[...]
    logits = [(0, logits_ref.shape[1], logits_ref[...])]
    current, _ = update(normal, logits, std_ref, old.astype(jnp.float32))
    new_ref[...] = current
    block_stats(current.astype(jnp.bfloat16), std_ref, stat_ref, next_ref)


def last_body(
    slab_rows, stats_ref, same_ref, swap_ref, logits_ref, std_ref, old_ref, new_ref, weight_ref
):
    normal = combine(stats_ref, same_ref, swap_ref, slab_rows)
    logits = [(0, logits_ref.shape[1], logits_ref[...])]
    current, weight = update(normal, logits, std_ref, old_ref[...])
    new_ref[...] = current
    flat = jnp.transpose(jnp.broadcast_to(weight, (weight.shape[0], LANES)))
    weight_ref[...] = flat[:1, :]


def spread(x):
    return lax.all_to_all(x, PEERS, split_axis=0, concat_axis=0, tiled=True)


def per_device(embeddings, coarse_lists, home, centroids):
    row_count, width = embeddings.shape
    peers = lax.axis_size(DP)
    total_rows = row_count * peers * lax.axis_size(("y", "x"))
    slabs, listed = coarse_lists.shape
    slab_rows = row_count // slabs
    most = 2
    cores = lax.axis_size(DP[-1])
    part = width // (2 * cores)
    slots = peers * most * slab_rows
    f32 = jnp.float32

    with jax.named_scope("sums_and_lists"):
        lists = coarse_lists.T
        payload = pl.pallas_call(
            lambda *refs: share_body(cores, *refs),
            out_shape=jax.ShapeDtypeStruct((peers, 2, part + LANES), jnp.bfloat16),
            in_specs=[pl.BlockSpec(memory_space=pltpu.SMEM)] + vmem(1),
            out_specs=vmem(1)[0],
        )(lists, embeddings)
        shared = spread(payload)

    with jax.named_scope("slabs_out"):
        outgoing = pl.pallas_call(
            lambda *refs: dispatch(slab_rows, most, peers, cores, *refs),
            out_shape=jax.ShapeDtypeStruct((slots, width), jnp.bfloat16),
            in_specs=[pl.BlockSpec(memory_space=pltpu.SMEM)] * 2 + vmem(1),
            out_specs=vmem(1)[0],
            scratch_shapes=[pltpu.SMEM((peers * (most + 1),), jnp.int32)],
        )(lists, home, embeddings)
        received = spread(outgoing.reshape(peers, most * slab_rows, width)).reshape(slots, width)

    with jax.named_scope("feature_scale"):
        total = jnp.sum(shared[:, :, :part].astype(f32), axis=0).reshape(-1, LANES)
        total = lax.psum(lax.psum(total, "x"), "y")
        total = lax.all_gather(total, DP[-1], tiled=True)
        scale = lax.rsqrt(total / total_rows + 1e-06)

    with jax.named_scope("slot_masks"):
        me = lax.axis_index(PEERS)
        ids = jnp.arange(peers, dtype=jnp.int32)
        lists_all = shared[:, 0, part : part + slabs * listed].astype(jnp.int32)
        home_of = jnp.sum(jnp.where(lists_all[:, :, None] == ids, peer_of(home[0], peers, cores), 0), axis=2)
        hits = jnp.any(home_of.reshape(peers, slabs, listed)[..., None] == ids, axis=2)
        order = jnp.arange(slabs)
        earlier = (order[None, :] < order[:, None])[None, :, :, None]
        before = jnp.sum(jnp.where(earlier & hits[:, None], 1, 0), axis=2)
        place = jnp.where(hits, before, -1)
        mine = jnp.sum(jnp.where(ids == me, place, 0), axis=2)
        turn = jnp.arange(most)
        chosen = mine[:, None, :] == turn[:, None]

        def lanes_of(wanted):
            found = chosen[..., None] & (place[:, None] == wanted[:, None, None])
            found = jnp.any(found, axis=2).astype(f32)
            found = found.transpose(2, 0, 1).reshape(peers, peers * most)
            return jnp.repeat(found, slab_rows, axis=1)

        same, swap = lanes_of(turn), lanes_of(1 - turn)

    block = centroids[0, 0]
    work = 2 * slots * block.shape[0] * width
    logits_shape = jax.ShapeDtypeStruct((block.shape[0], slots), f32)
    stat_shape = jax.ShapeDtypeStruct((peers, 1, slots), f32)
    block_shape = jax.ShapeDtypeStruct(block.shape, f32)
    with jax.named_scope("first_logits"):
        std, logits, stat = call(
            first_body,
            (jax.ShapeDtypeStruct((slots, width), jnp.bfloat16), logits_shape, stat_shape),
            vmem(5),
            work,
            4 << 20,
        )(received, scale, block, same, swap)
    old = block
    for turn_index in range(ITERS - 1):
        with jax.named_scope("stats_out"):
            stats = spread(stat)
        with jax.named_scope("middle_update"):
            old, logits, stat = call(
                lambda *refs: middle_body(slab_rows, *refs),
                (block_shape, logits_shape, stat_shape),
                vmem(6),
                2 * work,
                5 << 20,
            )(stats, same, swap, logits, std, old)
    with jax.named_scope("last_stats_out"):
        stats = spread(stat)
    with jax.named_scope("last_update"):
        current, weight = call(
            lambda *refs: last_body(slab_rows, *refs),
            (block_shape, jax.ShapeDtypeStruct((1, block.shape[0]), f32)),
            vmem(6),
            work,
            5 << 20,
        )(stats, same, swap, logits, std, old)
    return current[None, None], weight[None]


def solution(mesh):
    chips, rows = 12, 8
    cores = mesh.devices.shape[0] // chips
    grid = np.asarray(mesh.devices).reshape(chips // LOW, LOW, cores, rows, -1)
    fine = Mesh(grid, (*DP, "y", "x"))
    group = ("y", "x")
    return jax.shard_map(
        per_device,
        mesh=fine,
        in_specs=(P(DP + group, None), P(DP + group, None), P(group, None), P(group, DP, None, None)),
        out_specs=(P(group, DP, None, None), P(group, DP, None)),
        check_vma=False,
    )
```

```python
import math

import jax
import jax.numpy as jnp
import numpy as np
from jax import lax
from jax.experimental import pallas as pl
from jax.experimental.pallas import tpu as pltpu
from jax.sharding import Mesh, PartitionSpec as P

ITERS = 2
DP = ("z", "core")
PEERS = ("core", "z")
LANES = 128

prior_count = 1.0


def vmem(count):
    return [pl.BlockSpec(memory_space=pltpu.VMEM)] * count


def call(body, outs, specs, flops, moved):
    return pl.pallas_call(
        body,
        out_shape=outs,
        in_specs=specs,
        out_specs=tuple(vmem(len(outs))),
        compiler_params=pltpu.CompilerParams(vmem_limit_bytes=16 * 2**20),
        cost_estimate=pl.CostEstimate(flops=flops, bytes_accessed=moved, transcendentals=0),
    )


def peer_of(position, peers, cores):
    return (position % cores) * (peers // cores) + position // cores


def share_body(cores, lists_ref, emb_ref, out_ref):
    listed, slabs = lists_ref.shape
    wide = emb_ref[...].astype(jnp.float32)
    squares = jnp.sum(wide * wide, axis=0, keepdims=True)
    lane = lax.broadcasted_iota(jnp.int32, (1, LANES), 1)
    names = jnp.zeros((1, LANES), jnp.int32)
    for n in range(slabs * listed):
        names = jnp.where(lane == n, lists_ref[n % listed, n // listed], names)
    part = wide.shape[1] // (2 * cores)
    names = names.astype(jnp.float32)
    for core in range(cores):
        at = 2 * part * core
        upper = jnp.concatenate([squares[:, at : at + part], names], axis=1)
        lower = jnp.concatenate([squares[:, at + part : at + 2 * part], names], axis=1)
        payload = jnp.concatenate([upper, lower], axis=0).astype(jnp.bfloat16)
        for p in range(out_ref.shape[0] // cores):
            out_ref[core * (out_ref.shape[0] // cores) + p] = payload


def dispatch(slab_rows, most, peers, cores, lists_ref, home_ref, emb_ref, out_ref, table):
    listed, slabs = lists_ref.shape

    def clear(p, carry):
        table[p] = 0
        return carry

    lax.fori_loop(0, peers * most, clear, 0)

    def count_clear(p, carry):
        table[peers * most + p] = 0
        return carry

    lax.fori_loop(0, peers, count_clear, 0)

    def place(n, carry):
        slab, k = n // listed, n % listed
        p = peer_of(home_ref[0, lists_ref[k, slab]], peers, cores)
        seen = table[peers * most + p]
        table[p * most + jnp.minimum(seen, most - 1)] = slab
        table[peers * most + p] = seen + 1
        return carry

    lax.fori_loop(0, slabs * listed, place, 0)

    def copy(n, carry):
        source = pl.multiple_of(table[n] * slab_rows, slab_rows)
        target = pl.multiple_of(n * slab_rows, slab_rows)
        out_ref[pl.ds(target, slab_rows), :] = emb_ref[pl.ds(source, slab_rows), :]
        return carry

    lax.fori_loop(0, peers * most, copy, 0)


def block_logits(block_low, std_ref):
    width = block_low.shape[1]
    wide = block_low.astype(jnp.float32)
    cnorm = jnp.sum(wide * wide, axis=1, keepdims=True)
    chunk = 2 * LANES
    for c in range(0, std_ref.shape[0], chunk):
        products = lax.dot_general(
            block_low,
            std_ref[c : c + chunk, :],
            (((1,), (1,)), ((), ())),
            preferred_element_type=jnp.float32,
        )
        yield c, chunk, (2.0 * products - cnorm) * (1.0 / math.sqrt(width))


def block_stats(block_low, std_ref, stat_ref, logits_ref=None):
    lines = []
    for c, chunk, logits in block_logits(block_low, std_ref):
        if logits_ref is not None:
            logits_ref[:, c : c + chunk] = logits
        largest = jnp.max(logits, axis=0, keepdims=True)
        total = jnp.sum(jnp.exp(logits - largest), axis=0, keepdims=True)
        lines.append(largest + jnp.log(total))
    stat = jnp.concatenate(lines, axis=1)
    for p in range(stat_ref.shape[0]):
        stat_ref[p] = stat


def first_body(
    got_ref, scale_ref, block_ref, same_ref, swap_ref, std_ref, logits_ref, stat_ref
):
    chunk = 2 * LANES
    scale = jnp.concatenate([scale_ref[r : r + 1, :] for r in range(scale_ref.shape[0])], axis=1)
    for c in range(got_ref.shape[0] // chunk):
        at = slice(c * chunk, (c + 1) * chunk)
        std_ref[at, :] = (got_ref[at, :].astype(jnp.float32) * scale).astype(jnp.bfloat16)
    block_stats(block_ref[...], std_ref, stat_ref, logits_ref)


def combine(stats_ref, same_ref, swap_ref, slab_rows):
    lines = []
    for c in range(0, stats_ref.shape[2], LANES):
        own = stats_ref[:, 0, c : c + LANES]
        lane = lax.broadcasted_iota(jnp.int32, own.shape, 1)
        ahead = pltpu.roll(own, LANES - slab_rows, 1)
        behind = pltpu.roll(own, slab_rows, 1)
        other = jnp.where(lane % (2 * slab_rows) < slab_rows, ahead, behind)
        first = jnp.where(same_ref[:, c : c + LANES] > 0, own, -jnp.inf)
        second = jnp.where(swap_ref[:, c : c + LANES] > 0, other, -jnp.inf)
        summit = jnp.max(jnp.maximum(first, second), axis=0, keepdims=True)
        live = summit > -jnp.inf
        summit = jnp.where(live, summit, 0.0)
        total = jnp.sum(jnp.exp(first - summit) + jnp.exp(second - summit), axis=0, keepdims=True)
        lines.append(jnp.where(live, summit + jnp.log(jnp.where(live, total, 1.0)), jnp.inf))
    return jnp.concatenate(lines, axis=1)


def update(normal, logits, std_ref, old):
    parts = []
    for c, chunk, values in logits:
        parts.append(jnp.exp(values - normal[:, c : c + chunk]))
    resp = jnp.concatenate(parts, axis=1)
    weight = jnp.sum(resp, axis=1, keepdims=True)
    sums = lax.dot_general(
        resp.astype(jnp.bfloat16),
        std_ref[...],
        (((1,), (0,)), ((), ())),
        preferred_element_type=jnp.float32,
    )
    return (sums + old) / (weight + prior_count), weight


def middle_body(
    slab_rows,
    stats_ref,
    same_ref,
    swap_ref,
    logits_ref,
    std_ref,
    old_ref,
    new_ref,
    next_ref,
    stat_ref,
):
    normal = combine(stats_ref, same_ref, swap_ref, slab_rows)
    old = old_ref[...]
    logits = [(0, logits_ref.shape[1], logits_ref[...])]
    current, _ = update(normal, logits, std_ref, old.astype(jnp.float32))
    new_ref[...] = current
    block_stats(current.astype(jnp.bfloat16), std_ref, stat_ref, next_ref)


def last_body(
    slab_rows, stats_ref, same_ref, swap_ref, logits_ref, std_ref, old_ref, new_ref, weight_ref
):
    normal = combine(stats_ref, same_ref, swap_ref, slab_rows)
    logits = [(0, logits_ref.shape[1], logits_ref[...])]
    current, weight = update(normal, logits, std_ref, old_ref[...])
    new_ref[...] = current
    flat = jnp.transpose(jnp.broadcast_to(weight, (weight.shape[0], LANES)))
    weight_ref[...] = flat[:1, :]


def spread(x):
    return lax.all_to_all(x, PEERS, split_axis=0, concat_axis=0, tiled=True)


def per_device(embeddings, coarse_lists, home, centroids):
    row_count, width = embeddings.shape
    peers = lax.axis_size(DP)
    total_rows = row_count * peers * lax.axis_size(("y", "x"))
    slabs, listed = coarse_lists.shape
    slab_rows = row_count // slabs
    most = 2
    cores = lax.axis_size(DP[1])
    part = width // (2 * cores)
    slots = peers * most * slab_rows
    f32 = jnp.float32

    with jax.named_scope("sums_and_lists"):
        lists = coarse_lists.T
        payload = pl.pallas_call(
            lambda *refs: share_body(cores, *refs),
            out_shape=jax.ShapeDtypeStruct((peers, 2, part + LANES), jnp.bfloat16),
            in_specs=[pl.BlockSpec(memory_space=pltpu.SMEM)] + vmem(1),
            out_specs=vmem(1)[0],
        )(lists, embeddings)
        shared = spread(payload)

    with jax.named_scope("slabs_out"):
        outgoing = pl.pallas_call(
            lambda *refs: dispatch(slab_rows, most, peers, cores, *refs),
            out_shape=jax.ShapeDtypeStruct((slots, width), jnp.bfloat16),
            in_specs=[pl.BlockSpec(memory_space=pltpu.SMEM)] * 2 + vmem(1),
            out_specs=vmem(1)[0],
            scratch_shapes=[pltpu.SMEM((peers * (most + 1),), jnp.int32)],
        )(lists, home, embeddings)
        received = spread(outgoing.reshape(peers, most * slab_rows, width)).reshape(slots, width)

    with jax.named_scope("feature_scale"):
        total = jnp.sum(shared[:, :, :part].astype(f32), axis=0).reshape(-1, LANES)
        total = lax.psum(lax.psum(total, "x"), "y")
        total = lax.all_gather(total, DP[1], tiled=True)
        scale = lax.rsqrt(total / total_rows + 1e-06)

    with jax.named_scope("slot_masks"):
        me = lax.axis_index(PEERS)
        ids = jnp.arange(peers, dtype=jnp.int32)
        lists_all = shared[:, 0, part : part + slabs * listed].astype(jnp.int32)
        home_of = jnp.sum(jnp.where(lists_all[:, :, None] == ids, peer_of(home[0], peers, cores), 0), axis=2)
        hits = jnp.any(home_of.reshape(peers, slabs, listed)[..., None] == ids, axis=2)
        order = jnp.arange(slabs)
        earlier = (order[None, :] < order[:, None])[None, :, :, None]
        before = jnp.sum(jnp.where(earlier & hits[:, None], 1, 0), axis=2)
        place = jnp.where(hits, before, -1)
        mine = jnp.sum(jnp.where(ids == me, place, 0), axis=2)
        turn = jnp.arange(most)
        chosen = mine[:, None, :] == turn[:, None]

        def lanes_of(wanted):
            found = chosen[..., None] & (place[:, None] == wanted[:, None, None])
            found = jnp.any(found, axis=2).astype(f32)
            found = found.transpose(2, 0, 1).reshape(peers, peers * most)
            return jnp.repeat(found, slab_rows, axis=1)

        same, swap = lanes_of(turn), lanes_of(1 - turn)

    block = centroids[0, 0]
    work = 2 * slots * block.shape[0] * width
    logits_shape = jax.ShapeDtypeStruct((block.shape[0], slots), f32)
    stat_shape = jax.ShapeDtypeStruct((peers, 1, slots), f32)
    block_shape = jax.ShapeDtypeStruct(block.shape, f32)
    with jax.named_scope("first_logits"):
        std, logits, stat = call(
            first_body,
            (jax.ShapeDtypeStruct((slots, width), jnp.bfloat16), logits_shape, stat_shape),
            vmem(5),
            work,
            4 << 20,
        )(received, scale, block, same, swap)
    old = block
    for turn_index in range(ITERS - 1):
        with jax.named_scope("stats_out"):
            stats = spread(stat)
        with jax.named_scope("middle_update"):
            old, logits, stat = call(
                lambda *refs: middle_body(slab_rows, *refs),
                (block_shape, logits_shape, stat_shape),
                vmem(6),
                2 * work,
                5 << 20,
            )(stats, same, swap, logits, std, old)
    with jax.named_scope("last_stats_out"):
        stats = spread(stat)
    with jax.named_scope("last_update"):
        current, weight = call(
            lambda *refs: last_body(slab_rows, *refs),
            (block_shape, jax.ShapeDtypeStruct((1, block.shape[0]), f32)),
            vmem(6),
            work,
            5 << 20,
        )(stats, same, swap, logits, std, old)
    return current[None, None], weight[None]


def solution(mesh):
    chips, rows = 12, 8
    grid = np.asarray(mesh.devices).reshape(chips, mesh.devices.shape[0] // chips, rows, -1)
    fine = Mesh(grid, ("z", "core", "y", "x"))
    group = ("y", "x")
    return jax.shard_map(
        per_device,
        mesh=fine,
        in_specs=(P(DP + group, None), P(DP + group, None), P(group, None), P(group, DP, None, None)),
        out_specs=(P(group, DP, None, None), P(group, DP, None)),
        check_vma=False,
    )
```
